128 devices in a mesh: machine: 8 (over x, core), dev: 16 (over y, z).
Axes of the slice: x: 4, y: 4, z: 4, core: 2. Of those that a mesh axis runs over, the one named last changes fastest.
Arguments:
- embed: bfloat16 [786432, 128], P(('machine', 'dev'))
- cotangent: float32 [786432, 128], P(('machine', 'dev'))
- degrees: int32 [786432], P(('machine', 'dev')), may hold values from 16 to 256
- send_rows: int32 [128, 128, 32], P(('machine', 'dev')), may hold values from -1 to 6143, as said below
- inner_tiles: bfloat16 [6144, 4, 128, 128], P(('machine', 'dev')), may hold values from 0 to 1, as said below
- inner_src: int32 [6144, 4], P(('machine', 'dev')), may hold values from 0 to 47
- border_tiles: bfloat16 [6144, 4, 128, 128], P(('machine', 'dev')), may hold values from 0 to 1, as said below
- border_src: int32 [6144, 4], P(('machine', 'dev')), may hold values from 0 to 31
Outputs:
- final: bfloat16 [786432, 128], P(('machine', 'dev'))
- grad: float32 [786432, 128], P(('machine', 'dev'))
The draws below stay inside these ranges and needn't reach their ends.
Inputs may be any that keep to these rules, and one draw needn't show every extreme that they name: `send_rows`: -1 marks an empty slot; live slots of a pair come first. No partition sends to itself; every partition p fills all 32 slots for partition (p + 1) mod 128, and each other pair holds 1 to 32 live slots. `inner_tiles`: entries are 0 or 1. `border_tiles`: entries are 0 or 1.
All inputs are finite; a program needn't handle non-finite values.
Results may differ from the reference program's by a relative error of at most 0.002.
Values may be sent and summed in bfloat16 or wider, within the bound.
A program may use at most 128 MiB of HBM per device.

```python
import jax
import jax.numpy as jnp
from jax import lax

W = 128
BLK = 128
SLOT = 32
K_IN = 4
K_BD = 4
NB_DEV = 48
PEERS = 128
NODE_DEV = 6144
NODES = 786432
BLOCKS = 6144
RB = 32


def draw_embed(key, part):
    key = jax.random.fold_in(key, 11)
    key_mean, key_noise = jax.random.split(key, 2)
    column_mean = jax.random.uniform(key_mean, (1, W), jnp.float32, -1.5, 1.5)
    values = column_mean + jax.random.normal(key_noise, (NODES, W), jnp.float32)
    return jnp.clip(values, -8.0, 8.0).astype(jnp.bfloat16)


def draw_cotangent(key, part):
    key = jax.random.fold_in(key, 23)
    key_mean, key_noise = jax.random.split(key, 2)
    column_mean = jax.random.uniform(key_mean, (1, W), jnp.float32, -1.5, 1.5)
    values = column_mean + jax.random.normal(key_noise, (NODES, W), jnp.float32)
    return jnp.clip(values, -8.0, 8.0).astype(jnp.float32)


def draw_send_rows(key, part):
    key = jax.random.fold_in(key, 37)
    key_rows, key_count = jax.random.split(key, 2)
    row_index = jax.random.randint(key_rows, (PEERS, PEERS, SLOT), 0, NODE_DEV, jnp.int32)
    counts = jax.random.randint(key_count, (PEERS, PEERS, 1), 1, SLOT + 1, jnp.int32)
    sender = jnp.arange(PEERS, dtype=jnp.int32)[:, None, None]
    target = jnp.arange(PEERS, dtype=jnp.int32)[None, :, None]
    counts = jnp.where(target == (sender + 1) % PEERS, SLOT, counts)
    counts = jnp.where(target == sender, 0, counts)
    position = jnp.arange(SLOT, dtype=jnp.int32)[None, None, :]
    return jnp.where(position < counts, row_index, -1).astype(jnp.int32)


def draw_inner_tiles(key, part):
    key = jax.random.fold_in(key, 41)
    picks = jax.random.randint(key, (BLOCKS, K_IN, BLK, BLK), 0, 16, jnp.int32)
    return (picks == 0).astype(jnp.float32).astype(jnp.bfloat16)


def draw_border_tiles(key, part):
    key = jax.random.fold_in(key, 53)
    picks = jax.random.randint(key, (BLOCKS, K_BD, BLK, BLK), 0, 16, jnp.int32)
    return (picks == 0).astype(jnp.float32).astype(jnp.bfloat16)


def touch_ends(values, own_key, smallest, high):
    longest = values.shape.index(max(values.shape))
    spots = []
    for shift in (0, 1):
        where = [jax.random.randint(jax.random.fold_in(own_key, axis), (), 0, length) for axis, length in enumerate(values.shape)]
        where[longest] = (where[longest] + shift) % values.shape[longest]
        spots.append(tuple(where))
    return values.at[spots[0]].set(smallest).at[spots[1]].set(high)


def setup_inputs(seed: int = 0) -> dict:
    splits = jax.random.split(jax.random.key(seed), 9)
    embed = draw_embed(jax.random.fold_in(splits[8], 71), 0)
    cotangent = draw_cotangent(jax.random.fold_in(splits[8], 71), 0)
    degrees = touch_ends(jax.random.randint(splits[2], (NODES,), 16, 257), jax.random.fold_in(splits[2], 1), 16, 256).astype(jnp.int32)
    send_rows = draw_send_rows(jax.random.fold_in(splits[8], 71), 0)
    inner_tiles = draw_inner_tiles(jax.random.fold_in(splits[8], 71), 0)
    inner_src = touch_ends(jax.random.randint(splits[5], (BLOCKS, K_IN), 0, NB_DEV), jax.random.fold_in(splits[5], 1), 0, NB_DEV - 1).astype(jnp.int32)
    border_tiles = draw_border_tiles(jax.random.fold_in(splits[8], 71), 0)
    border_src = touch_ends(jax.random.randint(splits[7], (BLOCKS, K_BD), 0, RB), jax.random.fold_in(splits[7], 1), 0, RB - 1).astype(jnp.int32)
    return {"embed": embed, "cotangent": cotangent, "degrees": degrees, "send_rows": send_rows, "inner_tiles": inner_tiles, "inner_src": inner_src, "border_tiles": border_tiles, "border_src": border_src}


def make_hop(send_rows, inner_tiles, inner_src, border_tiles, border_src):
    inner_all = inner_tiles.reshape(PEERS, NB_DEV, K_IN, BLK, BLK)
    inner_idx = inner_src.reshape(PEERS, NB_DEV, K_IN)
    border_all = border_tiles.reshape(PEERS, NB_DEV, K_BD, BLK, BLK)
    border_idx = border_src.reshape(PEERS, NB_DEV, K_BD)
    sender_ids = jnp.arange(PEERS, dtype=jnp.int32)[:, None]

    def apply_hop(field):
        table = field.reshape(PEERS, NODE_DEV, W)

        def one_partition(target):
            column = lax.dynamic_index_in_dim(send_rows, target, 1, keepdims=False)
            live_mask = (column >= 0)[:, :, None]
            row_index = jnp.maximum(column, 0)
            arrived = jnp.where(live_mask, table[sender_ids, row_index], 0.0)
            received = arrived.reshape(RB, BLK, W)
            own_blocks = lax.dynamic_index_in_dim(table, target, 0, keepdims=False).reshape(NB_DEV, BLK, W)
            tiles_in = lax.dynamic_index_in_dim(inner_all, target, 0, keepdims=False).astype(jnp.float32)
            tiles_bd = lax.dynamic_index_in_dim(border_all, target, 0, keepdims=False).astype(jnp.float32)
            idx_in = lax.dynamic_index_in_dim(inner_idx, target, 0, keepdims=False)
            idx_bd = lax.dynamic_index_in_dim(border_idx, target, 0, keepdims=False)
            inside = jnp.einsum('bkij,bkjw->biw', tiles_in, own_blocks[idx_in], precision=lax.Precision.HIGHEST)
            border_sum = jnp.einsum('bkij,bkjw->biw', tiles_bd, received[idx_bd], precision=lax.Precision.HIGHEST)
            return (inside + border_sum).reshape(NODE_DEV, W)
        result = lax.map(one_partition, jnp.arange(PEERS, dtype=jnp.int32))
        return result.reshape(NODES, W)
    return apply_hop

def to_bf16_value(value):
    rounded = lax.optimization_barrier(value.astype(jnp.bfloat16))
    return rounded.astype(jnp.float32)

def reference(embed, cotangent, degrees, send_rows, inner_tiles, inner_src, border_tiles, border_src):
    apply_hop = make_hop(send_rows, inner_tiles, inner_src, border_tiles, border_src)
    inv_root = lax.rsqrt(degrees.astype(jnp.float32))[:, None]
    embed_full = embed.astype(jnp.float32)
    first_in = to_bf16_value(inv_root * embed_full)
    hop_one = inv_root * apply_hop(first_in)
    second_in = to_bf16_value(inv_root * hop_one)
    hop_two = inv_root * apply_hop(second_in)
    final = ((embed_full + hop_one + hop_two) / 3.0).astype(jnp.bfloat16)
    unused, transpose_fn = jax.vjp(apply_hop, first_in)
    first_back = to_bf16_value(inv_root * cotangent)
    back_one = inv_root * transpose_fn(first_back)[0]
    second_back = to_bf16_value(inv_root * back_one)
    back_two = inv_root * transpose_fn(second_back)[0]
    grad = (cotangent + back_one + back_two) / 3.0
    return (final, grad)
```

```python
import jax
import jax.numpy as jnp
import functools

from jax import lax
from jax.experimental import pallas as pl
from jax.experimental.pallas import tpu as pltpu
from jax.sharding import PartitionSpec as P


def _exchange_kernel(machines, devs, src_ref, dst_ref, send_sem, recv_sem):
    my_m = lax.axis_index("machine")
    my_d = lax.axis_index("dev")
    me = my_m * devs + my_d
    count = machines * devs

    def peer(step):
        offset = (step * 37) % count
        pm = (my_m + offset // devs) % machines
        pd = (my_d + offset % devs) % devs
        return pm, pd

    barrier = pltpu.get_barrier_semaphore()

    def greet(step, carry):
        pl.semaphore_signal(barrier, inc=1, device_id=peer(step), device_id_type=pl.DeviceIdType.MESH)
        return carry

    lax.fori_loop(1, count, greet, 0)
    pl.semaphore_wait(barrier, count - 1)

    def send(step, carry):
        pm, pd = peer(step)
        pltpu.make_async_remote_copy(
            src_ref=src_ref.at[pm * devs + pd],
            dst_ref=dst_ref.at[me],
            send_sem=send_sem,
            recv_sem=recv_sem,
            device_id=(pm, pd),
            device_id_type=pl.DeviceIdType.MESH,
        ).start()
        return carry

    lax.fori_loop(1, count, send, 0)
    dst_ref[pl.ds(me, 1)] = jnp.zeros((1,) + dst_ref.shape[1:], dst_ref.dtype)
    most = dst_ref.at[pl.ds(0, count - 1)]
    pltpu.make_async_copy(most, most, recv_sem).wait()
    sent = src_ref.at[pl.ds(0, count - 1)]
    pltpu.make_async_copy(sent, sent, send_sem).wait()


def exchange(outgoing, machines, devs):
    return pl.pallas_call(
        functools.partial(_exchange_kernel, machines, devs),
        out_shape=jax.ShapeDtypeStruct(outgoing.shape, outgoing.dtype),
        in_specs=[pl.BlockSpec(memory_space=pltpu.VMEM)],
        out_specs=pl.BlockSpec(memory_space=pltpu.VMEM),
        scratch_shapes=[pltpu.SemaphoreType.DMA, pltpu.SemaphoreType.DMA],
        compiler_params=pltpu.CompilerParams(
            collective_id=0, has_side_effects=True, vmem_limit_bytes=16 * 2**20
        ),
        name="exchange",
    )(outgoing)


def per_device(
    embed, cotangent, degrees, send_rows, inner_tiles, inner_src, border_tiles, border_src
):
    machines = lax.axis_size("machine")
    devs = lax.axis_size("dev")
    inv_root = lax.rsqrt(degrees.astype(jnp.float32))[:, None]
    table = send_rows[0]
    peer_count = table.shape[0]
    slot_count = table.shape[1]
    feature_width = embed.shape[1]
    block_rows = inner_tiles.shape[2]
    local_blocks = embed.shape[0] // block_rows
    border_blocks = peer_count * slot_count // block_rows
    live_mask = (table >= 0)[:, :, None]
    row_index = jnp.maximum(table, 0)
    flat_index = row_index.reshape(-1)
    inner_pick = (
        inner_src[:, :, None] == jnp.arange(local_blocks, dtype=jnp.int32)[None, None, :]
    ).astype(jnp.float32)
    border_pick = (
        border_src[:, :, None] == jnp.arange(border_blocks, dtype=jnp.int32)[None, None, :]
    ).astype(jnp.float32)

    def fetch_rows(field):
        outgoing = jnp.where(live_mask, field[row_index], jnp.zeros((), field.dtype))
        arrived = exchange(outgoing, machines, devs)
        return arrived.reshape(-1, block_rows, feature_width)

    def push_grads(border_grad):
        outgoing = border_grad.reshape(peer_count, slot_count, feature_width)
        arrived = exchange(outgoing.astype(jnp.bfloat16), machines, devs).astype(outgoing.dtype)
        return jnp.where(live_mask, arrived, 0.0).reshape(-1, feature_width)

    def forward_hop(field):
        received = fetch_rows(field)
        own_blocks = field.reshape(-1, block_rows, feature_width)
        inside = jnp.einsum(
            "bkij,bkjw->biw", inner_tiles, own_blocks[inner_src], preferred_element_type=jnp.float32
        )
        border_sum = jnp.einsum(
            "bkij,bkjw->biw", border_tiles, received[border_src], preferred_element_type=jnp.float32
        )
        return (inside + border_sum).reshape(-1, feature_width)

    def backward_hop(upstream):
        up_blocks = upstream.reshape(-1, block_rows, feature_width)
        to_border = jnp.einsum(
            "bkij,biw->bkjw", border_tiles, up_blocks, preferred_element_type=jnp.float32
        )
        border_grad = jnp.einsum(
            "bkr,bkjw->rjw",
            border_pick,
            to_border,
            precision=lax.Precision.HIGHEST,
            preferred_element_type=jnp.float32,
        )
        returned = push_grads(border_grad)
        to_inside = jnp.einsum(
            "bkij,biw->bkjw", inner_tiles, up_blocks, preferred_element_type=jnp.float32
        )
        local_grad = jnp.einsum(
            "bkc,bkjw->cjw",
            inner_pick,
            to_inside,
            precision=lax.Precision.HIGHEST,
            preferred_element_type=jnp.float32,
        )
        local_grad = local_grad.reshape(-1, feature_width)
        return local_grad.at[flat_index].add(returned)

    embed_full = embed.astype(jnp.float32)
    first_in = (inv_root * embed_full).astype(jnp.bfloat16)
    hop_one = inv_root * forward_hop(first_in)
    second_in = (inv_root * hop_one).astype(jnp.bfloat16)
    hop_two = inv_root * forward_hop(second_in)
    final = ((embed_full + hop_one + hop_two) / 3.0).astype(jnp.bfloat16)
    first_back = (inv_root * cotangent).astype(jnp.bfloat16)
    back_one = inv_root * backward_hop(first_back)
    second_back = (inv_root * back_one).astype(jnp.bfloat16)
    back_two = inv_root * backward_hop(second_back)
    grad = (cotangent + back_one + back_two) / 3.0
    return (final, grad)


def solution(mesh):
    in_specs = (
        P(("machine", "dev"), None),
        P(("machine", "dev"), None),
        P(("machine", "dev")),
        P(("machine", "dev"), None, None),
        P(("machine", "dev"), None, None, None),
        P(("machine", "dev"), None),
        P(("machine", "dev"), None, None, None),
        P(("machine", "dev"), None),
    )
    out_specs = (P(("machine", "dev"), None), P(("machine", "dev"), None))
    return jax.shard_map(
        per_device, mesh=mesh, in_specs=in_specs, out_specs=out_specs, check_vma=False
    )
```

```python
import functools

import jax
import jax.numpy as jnp
from jax import lax
from jax.experimental import pallas as pl
from jax.experimental.pallas import tpu as pltpu
from jax.sharding import PartitionSpec as P

F32 = jnp.float32
BF16 = jnp.bfloat16
THIRD = 1.0 / 3.0
TRANS = (((0,), (0,)), ((), ()))
ANY = pl.BlockSpec(memory_space=pl.ANY)
VM = pl.BlockSpec(memory_space=pltpu.VMEM)
SM = pl.BlockSpec(memory_space=pltpu.SMEM)


def rows_at(index, size):
    return pl.ds(pl.multiple_of(index * size, size), size)


def gather_rows(pick, table_ref, store, count, group=32):
    sub = lax.broadcasted_iota(jnp.int32, (8, 128), 0)

    def body(p, carry):
        base = pl.multiple_of(p * group, group)
        parts = []
        for g in range(group // 8):
            part = jnp.broadcast_to(table_ref[pl.ds(pick[base + g * 8], 1), :], (8, 128))
            for r in range(1, 8):
                row = table_ref[pl.ds(pick[base + g * 8 + r], 1), :]
                part = jnp.where(sub == r, jnp.broadcast_to(row, (8, 128)), part)
            parts.append(part)
        store(p, jnp.concatenate(parts, axis=0))
        return carry

    lax.fori_loop(0, count // group, body, 0, unroll=2)


def transposed_tiles(tiles_ref, src_ref, field_ref, total_ref, blocks, per):
    def body(b, carry):
        block = field_ref[rows_at(b, 128), :]
        for k in range(per):
            where = rows_at(src_ref[b * per + k], 128)
            product = lax.dot_general(tiles_ref[b, k], block, TRANS, preferred_element_type=F32)
            total_ref[where, :] = total_ref[where, :] + product
        return carry

    lax.fori_loop(0, blocks, body, 0, unroll=16)


def zero_fill(ref, rows):
    def body(i, carry):
        ref[rows_at(i, 256), :] = jnp.zeros((256, 128), ref.dtype)
        return carry

    lax.fori_loop(0, rows // 256, body, 0)


def start_kernel(
    blocks, border_blocks, per, slots,
    pick, border_src, embed, cotangent, degrees, border_hbm,
    outgoing, root_out, x0_out, u0_out,
    tiles, root_row, table, grad_rows, sems,
):
    nodes = blocks * 128
    half = blocks // 2
    copies = [
        pltpu.make_async_copy(
            border_hbm.at[pl.ds(h * half, half)], tiles.at[pl.ds(h * half, half)], sems.at[h]
        )
        for h in range(2)
    ]
    for copy in copies:
        copy.start()
    root_row[...] = lax.rsqrt(degrees[...].astype(F32))

    def scale(b, carry):
        where = rows_at(b, 128)
        root = jnp.broadcast_to(root_row[pl.ds(b, 1), :], (128, 128)).T
        root_out[where, :] = root
        x0 = (root * embed[where, :].astype(F32)).astype(BF16)
        x0_out[where, :] = x0
        table[where, :] = x0.astype(F32)
        u0_out[where, :] = (root * cotangent[where, :]).astype(BF16)
        return carry

    lax.fori_loop(0, blocks, scale, 0, unroll=4)
    table[pl.ds(nodes, 8), :] = jnp.zeros((8, 128), F32)
    zero_fill(grad_rows, border_blocks * 128)

    def put(p, rows):
        outgoing[p, pl.ds(0, slots), :] = rows.astype(BF16)

    gather_rows(pick, table, put, border_blocks * 128)
    for copy in copies:
        copy.wait()
    transposed_tiles(tiles, border_src, u0_out, grad_rows, blocks, per)

    def cast(p, carry):
        outgoing[p, pl.ds(slots, slots), :] = grad_rows[rows_at(p, slots), :].astype(BF16)
        return carry

    lax.fori_loop(0, border_blocks * 128 // slots, cast, 0, unroll=8)


def spread_arrived(blocks, order, ends, nodes_ref, arrived, table, sorted_rows, total, slots):
    count = sorted_rows.shape[0]

    def widen(p, carry):
        table[rows_at(p, slots), :] = arrived[p, pl.ds(slots, slots), :].astype(F32)
        return carry

    lax.fori_loop(0, count // slots, widen, 0, unroll=8)

    def put(p, rows):
        sorted_rows[rows_at(p, slots), :] = rows.astype(BF16)

    gather_rows(order, table, put, count)
    lane_node = lax.broadcasted_iota(jnp.int32, (128, 128), 0)
    chunks = count // 128

    def merge(step, carry):
        c, d = carry
        hot = (nodes_ref[pl.ds(c, 1), :] == lane_node + d * 128).astype(F32).astype(BF16)
        part = jnp.dot(hot, sorted_rows[rows_at(c, 128), :], preferred_element_type=F32)
        where = rows_at(d, 128)
        total[where, :] = total[where, :] + part
        end = ends[jnp.minimum(d, blocks - 1)]
        block_done = end <= (c + 1) * 128
        return (
            jnp.minimum(jnp.where(block_done, c, c + 1), chunks - 1),
            jnp.minimum(jnp.where(block_done, d + 1, d), blocks),
        )

    steps = chunks + blocks
    lax.fori_loop(0, steps, merge, (jnp.int32(0), jnp.int32(0)), unroll=8)


def forward_blocks(blocks, per_in, per_bd, inner_src, border_src, inner, border, own, arrived, slots, finish):
    peers = 128 // slots

    def body(b, carry):
        sources = [own[rows_at(inner_src[b * per_in + k], 128), :] for k in range(per_in)]
        for k in range(per_bd):
            first = border_src[b * per_bd + k] * peers
            sources.append(arrived[pl.ds(first, peers), pl.ds(0, slots), :].reshape(128, 128))
        lhs = [inner[b, k] for k in range(per_in)] + [border[b, k] for k in range(per_bd)]
        finish(
            b,
            jnp.dot(
                jnp.concatenate(lhs, axis=1),
                jnp.concatenate(sources, axis=0),
                preferred_element_type=F32,
            ),
        )
        return carry

    lax.fori_loop(0, blocks, body, 0, unroll=16)


def load_tiles(inner_hbm, border_hbm, inner, border, sems):
    copies = [
        pltpu.make_async_copy(inner_hbm, inner, sems.at[0]),
        pltpu.make_async_copy(border_hbm, border, sems.at[1]),
    ]
    for copy in copies:
        copy.start()
    return copies


def middle_kernel(
    blocks, border_blocks, per_in, per_bd, slots,
    pick, order, ends, inner_src, border_src,
    arrived, nodes_ref, root_ref, x0, u0, inner_hbm, border_hbm,
    outgoing, hop_out, back_out, x1_out, u1_out,
    inner, border, table, sorted_rows, total, grad_rows, sems,
):
    nodes = blocks * 128
    count = border_blocks * 128
    copies = load_tiles(inner_hbm, border_hbm, inner, border, sems)
    zero_fill(total, nodes)
    zero_fill(grad_rows, count)
    spread_arrived(blocks, order, ends, nodes_ref, arrived, table, sorted_rows, total, slots)
    copies[0].wait()
    transposed_tiles(inner, inner_src, u0, total, blocks, per_in)

    def step_back(b, carry):
        where = rows_at(b, 128)
        root = root_ref[where, :]
        back = root * total[where, :]
        back_out[where, :] = back
        u1_out[where, :] = (root * back).astype(BF16)
        return carry

    lax.fori_loop(0, blocks, step_back, 0, unroll=4)
    copies[1].wait()
    transposed_tiles(border, border_src, u1_out, grad_rows, blocks, per_bd)

    def cast(p, carry):
        outgoing[p, pl.ds(slots, slots), :] = grad_rows[rows_at(p, slots), :].astype(BF16)
        return carry

    lax.fori_loop(0, count // slots, cast, 0, unroll=8)

    def finish(b, value):
        where = rows_at(b, 128)
        root = root_ref[where, :]
        hop = root * value
        hop_out[where, :] = hop
        x1 = (root * hop).astype(BF16)
        x1_out[where, :] = x1
        table[where, :] = x1.astype(F32)

    forward_blocks(
        blocks, per_in, per_bd, inner_src, border_src, inner, border, x0, arrived, slots, finish
    )
    table[pl.ds(nodes, 8), :] = jnp.zeros((8, 128), F32)

    def put(p, rows):
        outgoing[p, pl.ds(0, slots), :] = rows.astype(BF16)

    gather_rows(pick, table, put, count)


def end_kernel(
    blocks, border_blocks, per_in, per_bd, slots,
    order, ends, inner_src, border_src,
    arrived, nodes_ref, embed, cotangent, root_ref, hop_ref, back_ref, x1, u1, inner_hbm, border_hbm,
    final_out, grad_out,
    inner, border, table, sorted_rows, total, sems,
):
    nodes = blocks * 128
    copies = load_tiles(inner_hbm, border_hbm, inner, border, sems)
    zero_fill(total, nodes)
    spread_arrived(blocks, order, ends, nodes_ref, arrived, table, sorted_rows, total, slots)
    copies[0].wait()
    transposed_tiles(inner, inner_src, u1, total, blocks, per_in)

    def step_back(b, carry):
        where = rows_at(b, 128)
        back = root_ref[where, :] * total[where, :]
        grad_out[where, :] = (cotangent[where, :] + back_ref[where, :] + back) * THIRD
        return carry

    lax.fori_loop(0, blocks, step_back, 0, unroll=4)
    copies[1].wait()

    def finish(b, value):
        where = rows_at(b, 128)
        hop = root_ref[where, :] * value
        mean = (embed[where, :].astype(F32) + hop_ref[where, :] + hop) * THIRD
        final_out[where, :] = mean.astype(BF16)

    forward_blocks(
        blocks, per_in, per_bd, inner_src, border_src, inner, border, x1, arrived, slots, finish
    )


def per_device(
    embed, cotangent, degrees, send_rows, inner_tiles, inner_src, border_tiles, border_src
):
    rows = send_rows[0]
    peers, slots = rows.shape
    nodes, width = embed.shape
    blocks, per_in = inner_src.shape
    per_bd = border_src.shape[1]
    count = peers * slots
    border_blocks = count // 128
    params = pltpu.CompilerParams(vmem_limit_bytes=60 * 2**20)
    flat = rows.reshape(1, count)
    pick = jnp.where(flat < 0, nodes, flat).reshape(count)
    keys = jnp.where(flat < 0, 2 * nodes, flat) * count + lax.broadcasted_iota(
        jnp.int32, (1, count), 1
    )
    keys = lax.sort(keys, dimension=1)
    order = (keys % count).reshape(count)
    sorted_nodes = (keys // count).reshape(border_blocks, 128)
    limits = (jnp.arange(blocks, dtype=jnp.int32) + 1) * 128
    ends = jnp.sum((flat >= 0) & (flat < limits[:, None]), axis=1, dtype=jnp.int32)
    in_src = inner_src.reshape(-1)
    bd_src = border_src.reshape(-1)
    tile_in = pltpu.VMEM((blocks, per_in, 128, 128), BF16)
    tile_bd = pltpu.VMEM((blocks, per_bd, 128, 128), BF16)
    field32 = jax.ShapeDtypeStruct((nodes, width), F32)
    field16 = jax.ShapeDtypeStruct((nodes, width), BF16)
    packet = jax.ShapeDtypeStruct((peers, 2 * slots, width), BF16)

    def exchange(outgoing):
        return lax.all_to_all(outgoing, ("machine", "dev"), split_axis=0, concat_axis=0, tiled=True)

    outgoing, root, x0, u0 = pl.pallas_call(
        functools.partial(start_kernel, blocks, border_blocks, per_bd, slots),
        out_shape=(packet, field32, field16, field16),
        in_specs=[SM, SM, VM, VM, VM, ANY],
        out_specs=(VM,) * 4,
        scratch_shapes=[
            tile_bd,
            pltpu.VMEM((blocks, 128), F32),
            pltpu.VMEM((nodes + 8, width), F32),
            pltpu.VMEM((count, width), F32),
            pltpu.SemaphoreType.DMA((2,)),
        ],
        compiler_params=params,
        name="start",
    )(pick, bd_src, embed, cotangent, degrees.reshape(blocks, 128), border_tiles)
    arrived = exchange(outgoing)
    outgoing, hop_one, back_one, x1, u1 = pl.pallas_call(
        functools.partial(middle_kernel, blocks, border_blocks, per_in, per_bd, slots),
        out_shape=(packet, field32, field32, field16, field16),
        in_specs=[SM] * 5 + [VM] * 5 + [ANY] * 2,
        out_specs=(VM,) * 5,
        scratch_shapes=[
            tile_in,
            tile_bd,
            pltpu.VMEM((nodes + 8, width), F32),
            pltpu.VMEM((count, width), BF16),
            pltpu.VMEM((nodes + 128, width), F32),
            pltpu.VMEM((count, width), F32),
            pltpu.SemaphoreType.DMA((2,)),
        ],
        compiler_params=params,
        name="middle",
    )(pick, order, ends, in_src, bd_src, arrived, sorted_nodes, root, x0, u0, inner_tiles, border_tiles)
    arrived = exchange(outgoing)
    final, grad = pl.pallas_call(
        functools.partial(end_kernel, blocks, border_blocks, per_in, per_bd, slots),
        out_shape=(field16, field32),
        in_specs=[SM] * 4 + [VM] * 9 + [ANY] * 2,
        out_specs=(VM,) * 2,
        scratch_shapes=[
            tile_in,
            tile_bd,
            pltpu.VMEM((count, width), F32),
            pltpu.VMEM((count, width), BF16),
            pltpu.VMEM((nodes + 128, width), F32),
            pltpu.SemaphoreType.DMA((2,)),
        ],
        compiler_params=params,
        name="end",
    )(
        order, ends, in_src, bd_src, arrived, sorted_nodes, embed, cotangent, root, hop_one, back_one,
        x1, u1, inner_tiles, border_tiles,
    )
    return final, grad


def solution(mesh):
    both = ("machine", "dev")
    in_specs = (
        P(both, None),
        P(both, None),
        P(both),
        P(both, None, None),
        P(both, None, None, None),
        P(both, None),
        P(both, None, None, None),
        P(both, None),
    )
    out_specs = (P(both, None), P(both, None))
    return jax.shard_map(
        per_device, mesh=mesh, in_specs=in_specs, out_specs=out_specs, check_vma=False
    )
```

```python
import functools

import jax
import jax.numpy as jnp
from jax import lax
from jax.experimental import pallas as pl
from jax.experimental.pallas import tpu as pltpu
from jax.sharding import PartitionSpec as P

F32 = jnp.float32
BF16 = jnp.bfloat16
I32 = jnp.int32
THIRD = 1.0 / 3.0
TRANS = (((0,), (0,)), ((), ()))
LANES = (((1,), (1,)), ((), ()))
MESH = pl.DeviceIdType.MESH
ANY = pl.BlockSpec(memory_space=pl.ANY)
VM = pl.BlockSpec(memory_space=pltpu.VMEM)
SM = pl.BlockSpec(memory_space=pltpu.SMEM)
GROUPS = 64
DEAD = GROUPS - 1


def rows_at(index, size):
    return pl.ds(pl.multiple_of(index * size, size), size)


def iota(shape, axis):
    return lax.broadcasted_iota(I32, shape, axis)


def as_bf16(mask):
    return mask.astype(F32).astype(BF16)


def kept(flag, value):
    flags = jnp.broadcast_to(flag, value.shape)
    return jnp.where(flags > 0, value, 0.0)


def joined(flag, before, value):
    flags = jnp.broadcast_to(flag, value.shape)
    return jnp.where(flags > 0, before + value, value)


def group_ranks(groups, hot_ref, counted_ref):
    chunks = len(groups)
    row = iota((GROUPS, 128), 0)
    for c in range(chunks):
        hot_ref[c * GROUPS : (c + 1) * GROUPS, :] = as_bf16(groups[c] == row)
    before = as_bf16(iota((128, 128), 0) < iota((128, 128), 1))
    weights = jnp.concatenate([before, jnp.ones((128, 128), BF16)], axis=1)
    size = chunks * GROUPS
    counted_ref[:size, :] = jnp.dot(hot_ref[:size, :], weights, preferred_element_type=F32)
    total = jnp.zeros((GROUPS, 128), F32)
    for c in range(chunks):
        total = total + counted_ref[c * GROUPS : (c + 1) * GROUPS, 128:]
    lower = (iota((GROUPS, GROUPS), 1) < iota((GROUPS, GROUPS), 0)).astype(F32)
    start = jnp.dot(lower, total, precision=lax.Precision.HIGHEST, preferred_element_type=F32)
    running = start
    ranks = []
    later = []
    for c in range(chunks):
        part = slice(c * GROUPS, (c + 1) * GROUPS)
        hot = hot_ref[part, :].astype(F32)
        rank = jnp.sum(hot * (counted_ref[part, :128] + running), axis=0, keepdims=True)
        ranks.append(rank.astype(I32))
        later.append((rank > jnp.sum(hot * start, axis=0, keepdims=True)).astype(I32))
        running = running + counted_ref[part, 128:]
    return ranks, later, (start + total).astype(I32)


def place(ranks, rows, values):
    row = iota((rows, 128), 0)
    square = iota((128, 128), 0)
    placed = jnp.zeros((rows * len(values[0]), 128), F32)
    for rank, chunk_values in zip(ranks, values):
        high = (jnp.right_shift(rank, 7) == row).astype(F32)
        left = jnp.concatenate([high * value.astype(F32) for value in chunk_values], axis=0)
        right = as_bf16((rank & 127) == square)
        placed = placed + lax.dot_general(
            left.astype(BF16), right, LANES, preferred_element_type=F32
        )
    placed = placed.astype(I32)
    return [placed[i * rows : (i + 1) * rows] for i in range(len(values[0]))]


def split_table(table, chunks):
    parts = []
    first = 0
    for size in (chunks, chunks, 8, GROUPS, 24, GROUPS, 24, GROUPS):
        parts.append(table.at[pl.ds(first, size)])
        first += size
    return parts


def order_kernel(
    nodes, pers, slots_ref, sources_ref,
    table_out, nodes_out, hot_ref, counted_ref,
):
    chunks = slots_ref.shape[0]
    pick_out, order_out, path_out, stop_out, in_out, in_ends, bd_out, bd_ends = split_table(
        table_out, chunks
    )
    lane = iota((1, 128), 1)
    index = slots_ref[...]
    pick_out[...] = jnp.where(index < 0, nodes, index)
    low = index & 127
    high = jnp.where(index < 0, DEAD, jnp.right_shift(index, 7))
    groups = [high[c : c + 1] for c in range(chunks)]
    ranks, _, ends = group_ranks(groups, hot_ref, counted_ref)
    row = iota((GROUPS, 128), 0)
    step = iota((GROUPS, 128), 1)
    stop = row + jnp.maximum(jnp.right_shift(ends + 127, 7) - 1, 0)
    stop_out[...] = stop + 1
    live = row < nodes // 128
    passed = (live & (stop < step)).astype(F32)
    block = jnp.sum(passed, axis=0, keepdims=True).astype(I32)
    passed_before = (live & (stop < step - 1)).astype(F32)
    block_before = jnp.sum(passed_before, axis=0, keepdims=True).astype(I32)
    chunk = jnp.minimum(lane - block, chunks - 1)
    path_out[...] = jnp.concatenate(
        [chunk, block * 128, (block == block_before).astype(I32)] + [block] * 5, axis=0
    )
    values = [
        [jnp.full((1, 128), c, I32), lane, low[c : c + 1], groups[c]] for c in range(chunks)
    ]
    slot_chunk, slot_lane, node_low, node_high = place(ranks, chunks, values)
    order_out[...] = slot_chunk * 128 + slot_lane
    nodes_out[...] = node_high * 128 + node_low
    for part, out, out_ends in ((0, in_out, in_ends), (1, bd_out, bd_ends)):
        groups = [sources_ref[part * 2 + c : part * 2 + c + 1, :] for c in range(2)]
        ranks, later, ends = group_ranks(groups, hot_ref, counted_ref)
        before = jnp.concatenate([jnp.zeros((1, 128), I32), ends[:-1]], axis=0)
        out_ends[...] = jnp.where(iota((GROUPS, 128), 1) == 1, ends - before, ends)
        shift = pers[part].bit_length() - 1
        values = [
            [lane + c * 128, later[c], jnp.right_shift(lane + c * 128, shift)] for c in range(2)
        ]
        for i, placed in enumerate(place(ranks, 8, values)):
            out[i * 8 : i * 8 + 8, :] = placed


def hop_kernel(
    machines, devs, blocks, border_blocks, per_in, per_bd, slots,
    index_table, inner_src, border_src, nodes_ref, degrees, embed_hbm, cotangent_hbm, inner_hbm, border_hbm,
    final_ref, grad_ref,
    inner, border, run, table, root_ref, root_row, u, x, embed, total, mean, wide, sorted_rows,
    out_g0, out_g1, out_x0, out_x1, in_g0, in_g1, in_x0, in_x1, copy_sem, send_sem, recv_sem,
):
    nodes = blocks * 128
    peers = 128 // slots
    out_g, out_x, in_g, in_x = (out_g0, out_g1), (out_x0, out_x1), (in_g0, in_g1), (in_x0, in_x1)
    chunks = border_blocks
    pick, order, path, stop, in_order, in_ends, bd_order, bd_ends = split_table(index_table, chunks)
    count = machines * devs
    my_m = lax.axis_index("machine")
    my_d = lax.axis_index("dev")
    me = my_m * devs + my_d
    rows_of_devs = devs // peers

    copies = [
        pltpu.make_async_copy(src, dst, copy_sem.at[i])
        for i, (src, dst) in enumerate(
            (
                (cotangent_hbm, grad_ref),
                (border_hbm, border),
                (embed_hbm, embed),
                (inner_hbm, inner),
            )
        )
    ]
    for copy in copies:
        copy.start()

    barrier = pltpu.get_barrier_semaphore()

    def greet(step, carry):
        pm = (my_m + step // devs) % machines
        pd = (my_d + step % devs) % devs
        pl.semaphore_signal(barrier, inc=1, device_id=(pm, pd), device_id_type=MESH)
        return carry

    lax.fori_loop(1, count, greet, 0)
    for buffer in in_g:
        buffer[pl.ds(me, 1)] = jnp.zeros((1, slots, 128), BF16)
    for buffer in in_x:
        buffer[pl.ds(my_m * rows_of_devs + my_d // peers, 1), pl.ds(my_d % peers, 1)] = jnp.zeros((1, 1, slots, 128), BF16)

    def send_all(kind, hop, out_buffer, in_buffer, fill):
        out_ref = out_buffer[hop]
        in_ref = in_buffer[hop]
        if kind == 0:
            mine = in_ref.at[me]
        else:
            mine = in_ref.at[my_m * rows_of_devs + my_d // peers, my_d % peers]

        def step(j, carry):
            offset = (j * 13) % chunks
            pm = (my_m + offset // rows_of_devs) % machines
            pr = (my_d // peers + offset % rows_of_devs) % rows_of_devs
            chunk = pm * rows_of_devs + pr
            out_ref[pl.ds(chunk * peers, peers)] = fill(chunk).reshape(peers, slots, 128)
            for q in range(peers):
                pd = pr * peers + (my_d + q) % peers
                peer = pm * devs + pd

                @pl.when(peer != me)
                def _():
                    pltpu.make_async_remote_copy(
                        src_ref=out_ref.at[peer],
                        dst_ref=mine,
                        send_sem=send_sem.at[kind, hop],
                        recv_sem=recv_sem.at[kind, hop],
                        device_id=(pm, pd),
                        device_id_type=MESH,
                    ).start()

            return carry

        lax.fori_loop(0, chunks, step, 0)

    def wait_for(buffer, hop, sem):
        most = buffer[hop].at[pl.ds(0, count - 1)]
        pltpu.make_async_copy(most, most, sem).wait()

    def grouped_tiles(tiles, tile_order, per, field):
        def body(t, carry):
            row, lane = t // 128, t % 128
            tile = tile_order[row, lane]
            after = tile_order[8 + row, lane]
            block = field[tile_order[16 + row, lane]]
            product = lax.dot_general(tiles[tile], block, TRANS, preferred_element_type=F32)
            run[t + 1] = joined(after, run[t], product)
            return carry

        run[0] = jnp.zeros((128, 128), F32)
        lax.fori_loop(0, blocks * per, body, 0, unroll=16)

    def grouped_sum(tile_ends, c):
        return kept(tile_ends[c, 1], run[tile_ends[c, 0]])

    def send_sums(hop):
        grouped_tiles(border, bd_order, per_bd, u)
        if hop == 0:
            pl.semaphore_wait(barrier, count - 1)
        send_all(0, hop, out_g, in_g, lambda c: grouped_sum(bd_ends, c).astype(BF16))

    sub = iota((8, 128), 0)

    def gather_chunk(which, source, chunk):
        parts = []
        for g in range(16):
            part = None
            for r in range(8):
                row = source[pl.ds(which[chunk, g * 8 + r], 1), :]
                row = jnp.broadcast_to(row, (8, 128))
                part = row if part is None else jnp.where(sub == r, row, part)
            parts.append(part)
        return jnp.concatenate(parts, axis=0).astype(BF16)

    def send_rows(hop):
        send_all(1, hop, out_x, in_x, lambda c: gather_chunk(pick, table, c))

    def inner_back():
        grouped_tiles(inner, in_order, per_in, u)

        def body(c, carry):
            total[rows_at(c, 128), :] = grouped_sum(in_ends, c)
            return carry

        lax.fori_loop(0, blocks, body, 0, unroll=4)

    def inner_forward():
        def body(b, carry):
            lhs = jnp.concatenate([inner[b * per_in + k] for k in range(per_in)], axis=1)
            rhs = [x[inner_src[b * per_in + k]] for k in range(per_in)]
            table[rows_at(b, 128), :] = jnp.dot(
                lhs, jnp.concatenate(rhs, axis=0), preferred_element_type=F32
            )
            return carry

        lax.fori_loop(0, blocks, body, 0, unroll=16)

    def border_forward(hop, finish):
        wait_for(out_x, hop, recv_sem.at[1, hop])

        def body(b, carry):
            lhs = jnp.concatenate([border[b * per_bd + k] for k in range(per_bd)], axis=1)
            rhs = [
                in_x[hop][border_src[b * per_bd + k]].reshape(128, 128)
                for k in range(per_bd)
            ]
            value = jnp.dot(lhs, jnp.concatenate(rhs, axis=0), preferred_element_type=F32)
            where = rows_at(b, 128)
            finish(b, root_ref[where, :] * (table[where, :] + value))
            return carry

        lax.fori_loop(0, blocks, body, 0, unroll=16)

    def gather_back(hop, finish):
        wait_for(in_g, hop, recv_sem.at[0, hop])

        def widen(c, carry):
            rows = in_g[hop][pl.ds(c * peers, peers)].reshape(128, 128)
            wide[rows_at(c, 128), :] = rows.astype(F32)
            return carry

        lax.fori_loop(0, chunks, widen, 0, unroll=2)

        def sort_rows(c, carry):
            sorted_rows[c] = gather_chunk(order, wide, c)
            return carry

        lax.fori_loop(0, chunks, sort_rows, 0)
        square = iota((128, 128), 0)

        run[0] = jnp.zeros((128, 128), F32)

        def merge(step, carry):
            c = path[0, step]
            hot = as_bf16(nodes_ref[pl.ds(c, 1), :] == square + path[1, step])
            part = jnp.dot(hot, sorted_rows[c], preferred_element_type=F32)
            run[step + 1] = joined(path[2, step], run[step], part)
            return carry

        lax.fori_loop(0, chunks + blocks, merge, 0, unroll=8)

        def body(d, carry):
            where = rows_at(d, 128)
            finish(d, root_ref[where, :] * (total[where, :] + run[stop[d, 0]]))
            return carry

        lax.fori_loop(0, blocks, body, 0, unroll=4)

    root_row[...] = lax.rsqrt(degrees[...].astype(F32))
    copies[0].wait()

    def first_u(b, carry):
        where = rows_at(b, 128)
        root = jnp.broadcast_to(root_row[pl.ds(b, 1), :], (128, 128)).T
        root_ref[where, :] = root
        u[b] = (root * grad_ref[where, :]).astype(BF16)
        return carry

    lax.fori_loop(0, blocks, first_u, 0, unroll=4)
    copies[1].wait()
    send_sums(0)
    copies[2].wait()

    def first_x(b, carry):
        where = rows_at(b, 128)
        value = (root_ref[where, :] * embed[where, :].astype(F32)).astype(BF16)
        x[b] = value
        table[where, :] = value.astype(F32)
        return carry

    lax.fori_loop(0, blocks, first_x, 0, unroll=4)
    table[pl.ds(nodes, 8), :] = jnp.zeros((8, 128), F32)
    send_rows(0)
    copies[3].wait()
    inner_back()
    inner_forward()

    def next_u(b, back):
        where = rows_at(b, 128)
        grad_ref[where, :] = grad_ref[where, :] + back
        u[b] = (root_ref[where, :] * back).astype(BF16)

    gather_back(0, next_u)
    send_sums(1)

    def next_x(b, hop_one):
        where = rows_at(b, 128)
        mean[where, :] = embed[where, :].astype(F32) + hop_one
        value = (root_ref[where, :] * hop_one).astype(BF16)
        x[b] = value
        table[where, :] = value.astype(F32)

    border_forward(0, next_x)
    send_rows(1)
    inner_back()
    inner_forward()

    def end_u(b, back):
        where = rows_at(b, 128)
        grad_ref[where, :] = (grad_ref[where, :] + back) * THIRD

    gather_back(1, end_u)

    def end_x(b, hop_two):
        where = rows_at(b, 128)
        final_ref[where, :] = ((mean[where, :] + hop_two) * THIRD).astype(BF16)

    border_forward(1, end_x)
    for hop in range(2):
        wait_for(out_g, hop, send_sem.at[0, hop])
        wait_for(out_x, hop, send_sem.at[1, hop])


def per_device(
    embed, cotangent, degrees, send_rows, inner_tiles, inner_src, border_tiles, border_src
):
    peers, slots = send_rows.shape[1:]
    nodes, width = embed.shape
    blocks, per_in = inner_src.shape
    per_bd = border_src.shape[1]
    machines = lax.axis_size("machine")
    devs = lax.axis_size("dev")
    chunks = peers * slots // 128
    in_src = inner_src.reshape(-1)
    bd_src = border_src.reshape(-1)
    sources = jnp.stack([jnp.pad(s, (0, 256 - s.size), constant_values=DEAD) for s in (in_src, bd_src)])
    index_rows = 2 * chunks + 3 * GROUPS + 56
    index_table, sorted_nodes = pl.pallas_call(
        functools.partial(order_kernel, nodes, (per_in, per_bd)),
        out_shape=(
            jax.ShapeDtypeStruct((index_rows, 128), I32),
            jax.ShapeDtypeStruct((chunks, 128), I32),
        ),
        in_specs=[VM, VM],
        out_specs=(VM, VM),
        scratch_shapes=[
            pltpu.VMEM((chunks * GROUPS, 128), BF16),
            pltpu.VMEM((chunks * GROUPS, 256), F32),
        ],
        compiler_params=pltpu.CompilerParams(vmem_limit_bytes=16 * 2**20),
        name="order",
    )(send_rows.reshape(chunks, 128), sources.reshape(4, 128))

    buffer = pltpu.VMEM((peers, slots, width), BF16)
    by_row = pltpu.VMEM((chunks, 128 // slots, slots, width), BF16)
    final, grad = pl.pallas_call(
        functools.partial(
            hop_kernel, machines, devs, blocks, chunks, per_in, per_bd, slots
        ),
        out_shape=(
            jax.ShapeDtypeStruct((nodes, width), BF16),
            jax.ShapeDtypeStruct((nodes, width), F32),
        ),
        in_specs=[SM] * 3 + [VM] * 2 + [ANY] * 4,
        out_specs=(VM, VM),
        scratch_shapes=[
            pltpu.VMEM((blocks * per_in, 128, 128), BF16),
            pltpu.VMEM((blocks * per_bd, 128, 128), BF16),
            pltpu.VMEM((blocks * max(per_in, per_bd) + 1, 128, 128), F32),
            pltpu.VMEM((nodes + 8, width), F32),
            pltpu.VMEM((nodes, width), F32),
            pltpu.VMEM((blocks, 128), F32),
            pltpu.VMEM((blocks, 128, width), BF16),
            pltpu.VMEM((blocks, 128, width), BF16),
            pltpu.VMEM((nodes, width), BF16),
            pltpu.VMEM((nodes, width), F32),
            pltpu.VMEM((nodes, width), F32),
            pltpu.VMEM((chunks * 128, width), F32),
            pltpu.VMEM((chunks, 128, width), BF16),
            *([buffer] * 6),
            by_row,
            by_row,
            pltpu.SemaphoreType.DMA((4,)),
            pltpu.SemaphoreType.DMA((2, 2)),
            pltpu.SemaphoreType.DMA((2, 2)),
        ],
        compiler_params=pltpu.CompilerParams(
            collective_id=0, has_side_effects=True, vmem_limit_bytes=62 * 2**20
        ),
        name="hops",
    )(
        index_table, in_src, bd_src, sorted_nodes, degrees.reshape(blocks, 128), embed, cotangent,
        inner_tiles.reshape(-1, 128, 128), border_tiles.reshape(-1, 128, 128),
    )
    return final, grad


def solution(mesh):
    both = ("machine", "dev")
    in_specs = (
        P(both, None),
        P(both, None),
        P(both),
        P(both, None, None),
        P(both, None, None, None),
        P(both, None),
        P(both, None, None, None),
        P(both, None),
    )
    out_specs = (P(both, None), P(both, None))
    return jax.shard_map(
        per_device, mesh=mesh, in_specs=in_specs, out_specs=out_specs, check_vma=False
    )
```

```python
import functools

import jax
import jax.numpy as jnp
from jax import lax
from jax.experimental import pallas as pl
from jax.experimental.pallas import tpu as pltpu
from jax.sharding import PartitionSpec as P

F32 = jnp.float32
BF16 = jnp.bfloat16
I32 = jnp.int32
THIRD = 1.0 / 3.0
TRANS = (((0,), (0,)), ((), ()))
LANES = (((1,), (1,)), ((), ()))
MESH = pl.DeviceIdType.MESH
ANY = pl.BlockSpec(memory_space=pl.ANY)
VM = pl.BlockSpec(memory_space=pltpu.VMEM)
SM = pl.BlockSpec(memory_space=pltpu.SMEM)
GROUPS = 64
DEAD = GROUPS - 1


def rows_at(index, size):
    return pl.ds(pl.multiple_of(index * size, size), size)


def iota(shape, axis):
    return lax.broadcasted_iota(I32, shape, axis)


def as_bf16(mask):
    return mask.astype(F32).astype(BF16)


def kept(flag, value):
    flags = jnp.broadcast_to(flag, value.shape)
    return jnp.where(flags > 0, value, 0.0)


def joined(flag, before, value):
    flags = jnp.broadcast_to(flag, value.shape)
    return jnp.where(flags > 0, before + value, value)


def group_ranks(groups, hot_ref, counted_ref):
    chunks = len(groups)
    row = iota((GROUPS, 128), 0)
    for c in range(chunks):
        hot_ref[c * GROUPS : (c + 1) * GROUPS, :] = as_bf16(groups[c] == row)
    before = as_bf16(iota((128, 128), 0) < iota((128, 128), 1))
    weights = jnp.concatenate([before, jnp.ones((128, 128), BF16)], axis=1)
    size = chunks * GROUPS
    counted_ref[:size, :] = jnp.dot(hot_ref[:size, :], weights, preferred_element_type=F32)
    total = jnp.zeros((GROUPS, 128), F32)
    for c in range(chunks):
        total = total + counted_ref[c * GROUPS : (c + 1) * GROUPS, 128:]
    lower = (iota((GROUPS, GROUPS), 1) < iota((GROUPS, GROUPS), 0)).astype(F32)
    start = jnp.dot(lower, total, precision=lax.Precision.HIGHEST, preferred_element_type=F32)
    running = start
    ranks = []
    later = []
    for c in range(chunks):
        part = slice(c * GROUPS, (c + 1) * GROUPS)
        hot = hot_ref[part, :].astype(F32)
        rank = jnp.sum(hot * (counted_ref[part, :128] + running), axis=0, keepdims=True)
        ranks.append(rank.astype(I32))
        later.append((rank > jnp.sum(hot * start, axis=0, keepdims=True)).astype(I32))
        running = running + counted_ref[part, 128:]
    return ranks, later, (start + total).astype(I32)


def place(ranks, rows, values):
    row = iota((rows, 128), 0)
    square = iota((128, 128), 0)
    placed = jnp.zeros((rows * len(values[0]), 128), F32)
    for rank, chunk_values in zip(ranks, values):
        high = (jnp.right_shift(rank, 7) == row).astype(F32)
        left = jnp.concatenate([high * value.astype(F32) for value in chunk_values], axis=0)
        right = as_bf16((rank & 127) == square)
        placed = placed + lax.dot_general(
            left.astype(BF16), right, LANES, preferred_element_type=F32
        )
    placed = placed.astype(I32)
    return [placed[i * rows : (i + 1) * rows] for i in range(len(values[0]))]


def split_table(table, chunks):
    parts = []
    first = 0
    for size in (chunks, chunks, chunks, 8, GROUPS, 24, GROUPS, 24, GROUPS):
        parts.append(table.at[pl.ds(first, size)])
        first += size
    return parts


def order_kernel(
    nodes, pers, slots_ref, sources_ref,
    table_out, hot_ref, counted_ref,
):
    chunks = slots_ref.shape[0]
    nodes_out, pick_out, order_out, path_out, stop_out, in_out, in_ends, bd_out, bd_ends = split_table(
        table_out, chunks
    )
    lane = iota((1, 128), 1)
    index = slots_ref[...]
    pick_out[...] = jnp.where(index < 0, nodes, index)
    low = index & 127
    high = jnp.where(index < 0, DEAD, jnp.right_shift(index, 7))
    groups = [high[c : c + 1] for c in range(chunks)]
    ranks, _, ends = group_ranks(groups, hot_ref, counted_ref)
    row = iota((GROUPS, 128), 0)
    step = iota((GROUPS, 128), 1)
    stop = row + jnp.maximum(jnp.right_shift(ends + 127, 7) - 1, 0)
    stop_out[...] = stop + 1
    live = row < nodes // 128
    passed = (live & (stop < step)).astype(F32)
    block = jnp.sum(passed, axis=0, keepdims=True).astype(I32)
    passed_before = (live & (stop < step - 1)).astype(F32)
    block_before = jnp.sum(passed_before, axis=0, keepdims=True).astype(I32)
    chunk = jnp.minimum(lane - block, chunks - 1)
    path_out[...] = jnp.concatenate(
        [chunk, block * 128, (block == block_before).astype(I32)] + [block] * 5, axis=0
    )
    values = [
        [jnp.full((1, 128), c, I32), lane, low[c : c + 1], groups[c]] for c in range(chunks)
    ]
    slot_chunk, slot_lane, node_low, node_high = place(ranks, chunks, values)
    order_out[...] = slot_chunk * 128 + slot_lane
    nodes_out[...] = node_high * 128 + node_low
    for part, out, out_ends in ((0, in_out, in_ends), (1, bd_out, bd_ends)):
        groups = [sources_ref[part * 2 + c : part * 2 + c + 1, :] for c in range(2)]
        ranks, later, ends = group_ranks(groups, hot_ref, counted_ref)
        before = jnp.concatenate([jnp.zeros((1, 128), I32), ends[:-1]], axis=0)
        out_ends[...] = jnp.where(iota((GROUPS, 128), 1) == 1, ends - before, ends)
        shift = pers[part].bit_length() - 1
        values = [
            [lane + c * 128, later[c], jnp.right_shift(lane + c * 128, shift)] for c in range(2)
        ]
        for i, placed in enumerate(place(ranks, 8, values)):
            out[i * 8 : i * 8 + 8, :] = placed


def hop_kernel(
    machines, devs, blocks, border_blocks, per_in, per_bd, slots,
    index_table, inner_src, border_src, nodes_ref, degrees, embed_hbm, cotangent_hbm, inner_hbm, border_hbm,
    final_ref, grad_ref,
    inner, border, run, table, root_ref, root_row, u, x, embed, total, mean, wide, sorted_rows,
    out_g0, out_g1, out_x0, out_x1, in_g0, in_g1, in_x0, in_x1, copy_sem, send_sem, recv_sem,
):
    nodes = blocks * 128
    peers = 128 // slots
    out_g, out_x, in_g, in_x = (out_g0, out_g1), (out_x0, out_x1), (in_g0, in_g1), (in_x0, in_x1)
    chunks = border_blocks
    _, pick, order, path, stop, in_order, in_ends, bd_order, bd_ends = split_table(index_table, chunks)
    count = machines * devs
    my_m = lax.axis_index("machine")
    my_d = lax.axis_index("dev")
    me = my_m * devs + my_d
    rows_of_devs = devs // peers

    copies = [
        pltpu.make_async_copy(src, dst, copy_sem.at[i])
        for i, (src, dst) in enumerate(
            (
                (cotangent_hbm, grad_ref),
                (border_hbm, border),
                (embed_hbm, embed),
                (inner_hbm, inner),
            )
        )
    ]
    for copy in copies:
        copy.start()

    barrier = pltpu.get_barrier_semaphore()

    def greet(step, carry):
        pm = (my_m + step // devs) % machines
        pd = (my_d + step % devs) % devs
        pl.semaphore_signal(barrier, inc=1, device_id=(pm, pd), device_id_type=MESH)
        return carry

    lax.fori_loop(1, count, greet, 0)
    for buffer in in_g:
        buffer[pl.ds(me, 1)] = jnp.zeros((1, slots, 128), BF16)
    for buffer in in_x:
        buffer[pl.ds(my_m * rows_of_devs + my_d // peers, 1), pl.ds(my_d % peers, 1)] = jnp.zeros((1, 1, slots, 128), BF16)

    def send_all(kind, hop, out_buffer, in_buffer, fill):
        out_ref = out_buffer[hop]
        in_ref = in_buffer[hop]
        if kind == 0:
            mine = in_ref.at[me]
        else:
            mine = in_ref.at[my_m * rows_of_devs + my_d // peers, my_d % peers]

        def step(j, carry):
            offset = (j * 13) % chunks
            pm = (my_m + offset // rows_of_devs) % machines
            pr = (my_d // peers + offset % rows_of_devs) % rows_of_devs
            chunk = pm * rows_of_devs + pr
            out_ref[pl.ds(chunk * peers, peers)] = fill(chunk).reshape(peers, slots, 128)
            for q in range(peers):
                pd = pr * peers + (my_d + q) % peers
                peer = pm * devs + pd

                @pl.when(peer != me)
                def _():
                    pltpu.make_async_remote_copy(
                        src_ref=out_ref.at[peer],
                        dst_ref=mine,
                        send_sem=send_sem.at[kind, hop],
                        recv_sem=recv_sem.at[kind, hop],
                        device_id=(pm, pd),
                        device_id_type=MESH,
                    ).start()

            return carry

        lax.fori_loop(0, chunks, step, 0)

    def wait_for(buffer, hop, sem):
        most = buffer[hop].at[pl.ds(0, count - 1)]
        pltpu.make_async_copy(most, most, sem).wait()

    def grouped_tiles(tiles, tile_order, per, field):
        def body(t, carry):
            row, lane = t // 128, t % 128
            tile = tile_order[row, lane]
            after = tile_order[8 + row, lane]
            block = field[tile_order[16 + row, lane]]
            product = lax.dot_general(tiles[tile], block, TRANS, preferred_element_type=F32)
            run[t + 1] = joined(after, run[t], product)
            return carry

        run[0] = jnp.zeros((128, 128), F32)
        lax.fori_loop(0, blocks * per, body, 0, unroll=32)

    def grouped_sum(tile_ends, c):
        return kept(tile_ends[c, 1], run[tile_ends[c, 0]])

    def send_sums(hop):
        grouped_tiles(border, bd_order, per_bd, u)
        if hop == 0:
            pl.semaphore_wait(barrier, count - 1)
        send_all(0, hop, out_g, in_g, lambda c: grouped_sum(bd_ends, c).astype(BF16))

    sub = iota((8, 128), 0)

    def gather_chunk(which, source, chunk):
        parts = []
        for g in range(16):
            part = None
            for r in range(8):
                row = source[pl.ds(which[chunk, g * 8 + r], 1), :]
                row = jnp.broadcast_to(row, (8, 128))
                part = row if part is None else jnp.where(sub == r, row, part)
            parts.append(part)
        return jnp.concatenate(parts, axis=0).astype(BF16)

    def send_rows(hop):
        send_all(1, hop, out_x, in_x, lambda c: gather_chunk(pick, table, c))

    def inner_back():
        grouped_tiles(inner, in_order, per_in, u)

        def body(c, carry):
            total[rows_at(c, 128), :] = grouped_sum(in_ends, c)
            return carry

        lax.fori_loop(0, blocks, body, 0, unroll=8)

    def inner_forward():
        def body(b, carry):
            lhs = jnp.concatenate([inner[b * per_in + k] for k in range(per_in)], axis=1)
            rhs = [x[inner_src[b * per_in + k]] for k in range(per_in)]
            table[rows_at(b, 128), :] = jnp.dot(
                lhs, jnp.concatenate(rhs, axis=0), preferred_element_type=F32
            )
            return carry

        lax.fori_loop(0, blocks, body, 0, unroll=16)

    def border_forward(hop, finish):
        wait_for(out_x, hop, recv_sem.at[1, hop])

        def body(b, carry):
            lhs = jnp.concatenate([border[b * per_bd + k] for k in range(per_bd)], axis=1)
            rhs = [
                in_x[hop][border_src[b * per_bd + k]].reshape(128, 128)
                for k in range(per_bd)
            ]
            value = jnp.dot(lhs, jnp.concatenate(rhs, axis=0), preferred_element_type=F32)
            where = rows_at(b, 128)
            finish(b, root_ref[where, :] * (table[where, :] + value))
            return carry

        lax.fori_loop(0, blocks, body, 0, unroll=16)

    def gather_back(hop, finish):
        wait_for(in_g, hop, recv_sem.at[0, hop])

        def widen(c, carry):
            rows = in_g[hop][pl.ds(c * peers, peers)].reshape(128, 128)
            wide[rows_at(c, 128), :] = rows.astype(F32)
            return carry

        lax.fori_loop(0, chunks, widen, 0, unroll=4)

        def sort_rows(c, carry):
            sorted_rows[c] = gather_chunk(order, wide, c)
            return carry

        lax.fori_loop(0, chunks, sort_rows, 0)
        square = iota((128, 128), 0)

        run[0] = jnp.zeros((128, 128), F32)

        def merge(step, carry):
            c = path[0, step]
            hot = as_bf16(nodes_ref[pl.ds(c, 1), :] == square + path[1, step])
            part = jnp.dot(hot, sorted_rows[c], preferred_element_type=F32)
            run[step + 1] = joined(path[2, step], run[step], part)
            return carry

        lax.fori_loop(0, chunks + blocks, merge, 0, unroll=16)

        def body(d, carry):
            where = rows_at(d, 128)
            finish(d, root_ref[where, :] * (total[where, :] + run[stop[d, 0]]))
            return carry

        lax.fori_loop(0, blocks, body, 0, unroll=8)

    root_row[...] = lax.rsqrt(degrees[...].astype(F32))
    copies[0].wait()

    def first_u(b, carry):
        where = rows_at(b, 128)
        root = jnp.broadcast_to(root_row[pl.ds(b, 1), :], (128, 128)).T
        root_ref[where, :] = root
        u[b] = (root * grad_ref[where, :]).astype(BF16)
        return carry

    lax.fori_loop(0, blocks, first_u, 0, unroll=8)
    copies[1].wait()
    send_sums(0)
    copies[2].wait()

    def first_x(b, carry):
        where = rows_at(b, 128)
        value = (root_ref[where, :] * embed[where, :].astype(F32)).astype(BF16)
        x[b] = value
        table[where, :] = value.astype(F32)
        return carry

    lax.fori_loop(0, blocks, first_x, 0, unroll=8)
    table[pl.ds(nodes, 8), :] = jnp.zeros((8, 128), F32)
    send_rows(0)
    copies[3].wait()
    inner_back()
    inner_forward()

    def next_u(b, back):
        where = rows_at(b, 128)
        grad_ref[where, :] = grad_ref[where, :] + back
        u[b] = (root_ref[where, :] * back).astype(BF16)

    gather_back(0, next_u)
    send_sums(1)

    def next_x(b, hop_one):
        where = rows_at(b, 128)
        mean[where, :] = embed[where, :].astype(F32) + hop_one
        value = (root_ref[where, :] * hop_one).astype(BF16)
        x[b] = value
        table[where, :] = value.astype(F32)

    border_forward(0, next_x)
    send_rows(1)
    inner_back()
    inner_forward()

    def end_u(b, back):
        where = rows_at(b, 128)
        grad_ref[where, :] = (grad_ref[where, :] + back) * THIRD

    gather_back(1, end_u)

    def end_x(b, hop_two):
        where = rows_at(b, 128)
        final_ref[where, :] = ((mean[where, :] + hop_two) * THIRD).astype(BF16)

    border_forward(1, end_x)
    for hop in range(2):
        wait_for(out_g, hop, send_sem.at[0, hop])
        wait_for(out_x, hop, send_sem.at[1, hop])


def per_device(
    embed, cotangent, degrees, send_rows, inner_tiles, inner_src, border_tiles, border_src
):
    peers, slots = send_rows.shape[1:]
    nodes, width = embed.shape
    blocks, per_in = inner_src.shape
    per_bd = border_src.shape[1]
    machines = lax.axis_size("machine")
    devs = lax.axis_size("dev")
    chunks = peers * slots // 128
    in_src = inner_src.reshape(-1)
    bd_src = border_src.reshape(-1)
    sources = jnp.stack([jnp.pad(s, (0, 256 - s.size), constant_values=DEAD) for s in (in_src, bd_src)])
    index_rows = 3 * chunks + 3 * GROUPS + 56
    index_table = pl.pallas_call(
        functools.partial(order_kernel, nodes, (per_in, per_bd)),
        out_shape=jax.ShapeDtypeStruct((index_rows, 128), I32),
        in_specs=[VM, VM],
        out_specs=VM,
        scratch_shapes=[
            pltpu.VMEM((chunks * GROUPS, 128), BF16),
            pltpu.VMEM((chunks * GROUPS, 256), F32),
        ],
        compiler_params=pltpu.CompilerParams(vmem_limit_bytes=16 * 2**20),
        name="order",
    )(send_rows.reshape(chunks, 128), sources.reshape(4, 128))

    buffer = pltpu.VMEM((peers, slots, width), BF16)
    by_row = pltpu.VMEM((chunks, 128 // slots, slots, width), BF16)
    final, grad = pl.pallas_call(
        functools.partial(
            hop_kernel, machines, devs, blocks, chunks, per_in, per_bd, slots
        ),
        out_shape=(
            pltpu.VMEM((nodes, width), BF16),
            pltpu.VMEM((nodes, width), F32),
        ),
        in_specs=[SM] * 3 + [VM] * 2 + [ANY] * 4,
        out_specs=(VM, VM),
        scratch_shapes=[
            pltpu.VMEM((blocks * per_in, 128, 128), BF16),
            pltpu.VMEM((blocks * per_bd, 128, 128), BF16),
            pltpu.VMEM((blocks * max(per_in, per_bd) + 1, 128, 128), F32),
            pltpu.VMEM((nodes + 8, width), F32),
            pltpu.VMEM((nodes, width), F32),
            pltpu.VMEM((blocks, 128), F32),
            pltpu.VMEM((blocks, 128, width), BF16),
            pltpu.VMEM((blocks, 128, width), BF16),
            pltpu.VMEM((nodes, width), BF16),
            pltpu.VMEM((nodes, width), F32),
            pltpu.VMEM((nodes, width), F32),
            pltpu.VMEM((chunks * 128, width), F32),
            pltpu.VMEM((chunks, 128, width), BF16),
            *([buffer] * 6),
            by_row,
            by_row,
            pltpu.SemaphoreType.DMA((4,)),
            pltpu.SemaphoreType.DMA((2, 2)),
            pltpu.SemaphoreType.DMA((2, 2)),
        ],
        compiler_params=pltpu.CompilerParams(
            collective_id=0, has_side_effects=True, vmem_limit_bytes=56 * 2**20
        ),
        name="hops",
    )(
        index_table, in_src, bd_src, index_table, degrees.reshape(blocks, 128), embed, cotangent,
        inner_tiles.reshape(-1, 128, 128), border_tiles.reshape(-1, 128, 128),
    )
    return final, grad


def solution(mesh):
    both = ("machine", "dev")
    in_specs = (
        P(both, None),
        P(both, None),
        P(both),
        P(both, None, None),
        P(both, None, None, None),
        P(both, None),
        P(both, None, None, None),
        P(both, None),
    )
    out_specs = (P(both, None), P(both, None))
    return jax.shard_map(
        per_device, mesh=mesh, in_specs=in_specs, out_specs=out_specs, check_vma=False
    )
```
